128 devices in a mesh: gx: 4 (over z), gy: 8 (over x, y_lo), gz: 4 (over y_hi, core).
Axes of the slice: x: 4, y: 4 (y_hi: 2, y_lo: 2; y = y_hi * 2 + y_lo), z: 4, core: 2. Of those that a mesh axis runs over, the one named last changes fastest.
Arguments:
- tokens: bfloat16 [1024, 8192], P('gy', ('gx', 'gz')), may hold values from -6 to 6
- grad_out: bfloat16 [1024, 8192], P('gy', ('gx', 'gz')), may hold values from -6 to 6
- gate_pre: bfloat16 [1024, 14784], P(('gx', 'gz'), 'gy'), may hold values from -8 to 8
- up_pre: bfloat16 [1024, 14784], P(('gx', 'gz'), 'gy'), may hold values from -6 to 6
- gate_weight: bfloat16 [8192, 14784], P(('gx', 'gz'), 'gy'), may hold values from -0.0625 to 0.0625
- up_weight: bfloat16 [8192, 14784], P(('gx', 'gz'), 'gy'), may hold values from -0.0625 to 0.0625
- down_weight: bfloat16 [14784, 8192], P('gy', ('gx', 'gz')), may hold values from -0.046875 to 0.046875
Outputs:
- grad_tokens: bfloat16 [1024, 8192], P('gy', ('gx', 'gz'))
- grad_gate_weight: bfloat16 [8192, 14784], P(('gx', 'gz'), 'gy')
- grad_up_weight: bfloat16 [8192, 14784], P(('gx', 'gz'), 'gy')
- grad_down_weight: bfloat16 [14784, 8192], P('gy', ('gx', 'gz'))
The draws below stay inside these ranges and needn't reach their ends.
All inputs are finite; a program needn't handle non-finite values.
Results may differ from the reference program's by a relative error of at most 0.027.
Values may be sent and summed in bfloat16 or wider, within the bound.
A program may use at most 128 MiB of HBM per device.

```python
import jax
import jax.numpy as jnp
from jax import lax

D = 8192
FF = 14784
TOKENS = 1024
N_GX = 4
N_GY = 8
N_GZ = 4


def strengthened(entries, stream_key, source, target, parts, factor):
    owner, partner = [(jnp.arange(entries.shape[dim]) // (entries.shape[dim] // parts)).reshape([-1 if axis == dim else 1 for axis in range(entries.ndim)]) for dim in (source, target)]
    chosen = jax.random.permutation(stream_key, parts)[partner]
    strong = (owner == chosen) | (owner == (partner + parts // 2) % parts)
    return jnp.where(strong, factor * entries, entries)


def shard_levels(own_key, dims, cuts, least, top_value):
    factor_of, own = 1.0, jax.random.fold_in(own_key, 6)
    for axis_at, parts in cuts:
        draws = jnp.exp(jax.random.uniform(jax.random.fold_in(own, axis_at), (parts,), jnp.float32, least / len(cuts), top_value / len(cuts)))
        factor_of = factor_of * jnp.repeat(draws, dims[axis_at] // parts).reshape([-1 if axis == axis_at else 1 for axis in range(len(dims))])
    return factor_of


def bell_draw(own_key, extent, scale, bound, shards=(), held_as=jnp.bfloat16):
    entries = scale * jax.random.normal(own_key, extent, jnp.float32)
    if shards:
        entries = entries * shard_levels(own_key, extent, shards, -0.22, 0.18)
    return jnp.clip(entries, -bound, bound).astype(held_as)


def gaussian_with(rng, dims, deviation, bound, pieces, heavy, kind=jnp.bfloat16):
    array = deviation * jax.random.normal(rng, dims, jnp.float32)
    if pieces:
        array = array * shard_levels(rng, dims, pieces, -0.22, 0.18)
    return jnp.clip(strengthened(array, jax.random.fold_in(rng, 3), *heavy), -bound, bound).astype(kind)


def setup_inputs(seed: int = 0) -> dict:
    key_list = jax.random.split(jax.random.key(seed), 8)
    tokens = bell_draw(key_list[0], (TOKENS, D), 1.0, 6.0, ((0, 8), (1, 16)))
    grad_out = gaussian_with(key_list[1], (TOKENS, D), 1.0, 6.0, ((0, 8), (1, 16)), (1, 0, 16, 2.0))
    gate_pre = bell_draw(key_list[2], (TOKENS, FF), 1.5, 8.0, ((0, 16), (1, 8)))
    up_pre = gaussian_with(key_list[3], (TOKENS, FF), 1.0, 6.0, ((0, 16), (1, 8)), (1, 0, 16, 2.0))
    gate_weight = bell_draw(key_list[4], (D, FF), D ** -0.5, 0.0625, ((0, 16), (1, 8)))
    up_weight = bell_draw(key_list[5], (D, FF), D ** -0.5, 0.0625, ((0, 16), (1, 8)))
    down_weight = bell_draw(key_list[6], (FF, D), FF ** -0.5, 0.046875, ((0, 8), (1, 16)))
    return {"tokens": tokens, "grad_out": grad_out, "gate_pre": gate_pre, "up_pre": up_pre, "gate_weight": gate_weight, "up_weight": up_weight, "down_weight": down_weight}


def activation_grads(hidden_grad, gate_pre, up_pre):
    gate_value = gate_pre.astype(jnp.float32)
    up_value = up_pre.astype(jnp.float32)
    sigmoid_gate = jax.nn.sigmoid(gate_value)
    grad_gate_pre = (hidden_grad * up_value * sigmoid_gate * (1.0 + gate_value * (1.0 - sigmoid_gate))).astype(jnp.bfloat16)
    grad_up_pre = (hidden_grad * gate_value * sigmoid_gate).astype(jnp.bfloat16)
    hidden = (gate_value * sigmoid_gate * up_value).astype(jnp.bfloat16)
    return (grad_gate_pre, grad_up_pre, hidden)

def reference(tokens, grad_out, gate_pre, up_pre, gate_weight, up_weight, down_weight):
    blocks = N_GX * N_GZ
    piece_width = D // blocks
    hidden_grad = jnp.zeros((TOKENS, FF), jnp.float32)
    for number in range(blocks):
        lower = number * piece_width
        partial_value = jnp.dot(grad_out[:, lower:lower + piece_width], down_weight[:, lower:lower + piece_width].T, preferred_element_type=jnp.float32)
        hidden_grad = hidden_grad + lax.optimization_barrier(partial_value.astype(jnp.bfloat16)).astype(jnp.float32)
    grad_gate_pre, grad_up_pre, hidden = activation_grads(hidden_grad, gate_pre, up_pre)
    hidden_width = FF // N_GY
    input_total = jnp.zeros((TOKENS, D), jnp.float32)
    for number in range(N_GY):
        lower = number * hidden_width
        partial_value = jnp.dot(grad_gate_pre[:, lower:lower + hidden_width], gate_weight[:, lower:lower + hidden_width].T, preferred_element_type=jnp.float32)
        partial_value = partial_value + jnp.dot(grad_up_pre[:, lower:lower + hidden_width], up_weight[:, lower:lower + hidden_width].T, preferred_element_type=jnp.float32)
        input_total = input_total + lax.optimization_barrier(partial_value.astype(jnp.bfloat16)).astype(jnp.float32)
    grad_tokens = input_total.astype(jnp.bfloat16)
    grad_scale = 1.0 / jnp.sqrt(jnp.float32(TOKENS))
    grad_gate_weight = (jnp.dot(tokens.T, grad_gate_pre, preferred_element_type=jnp.float32) * grad_scale).astype(jnp.bfloat16)
    grad_up_weight = (jnp.dot(tokens.T, grad_up_pre, preferred_element_type=jnp.float32) * grad_scale).astype(jnp.bfloat16)
    grad_down_weight = (jnp.dot(hidden.T, grad_out, preferred_element_type=jnp.float32) * grad_scale).astype(jnp.bfloat16)
    return (grad_tokens, grad_gate_weight, grad_up_weight, grad_down_weight)
```

```python
import functools
import math

import jax
import jax.numpy as jnp
from jax import lax
from jax.experimental import pallas as pl
from jax.experimental.pallas import tpu as pltpu
from jax.sharding import PartitionSpec as P

MESH = pl.DeviceIdType.MESH
F32 = jnp.float32
BF16 = jnp.bfloat16
FB = 1848
DB = 512
LANES = ((0, 512), (512, 1024), (1024, 1536), (1536, 1848))
N_REMOTE = 96
SCALE = 1.0 / 32.0


def nt(a, b):
    return lax.dot_general(a, b, (((1,), (1,)), ((), ())), preferred_element_type=F32)


def tn(a, b):
    return lax.dot_general(a, b, (((0,), (0,)), ((), ())), preferred_element_type=F32)


def kernel(
    tok_in, go_in, gate_in, up_in, wg_in, wu_in, dw_in,
    gt_out, dwg_out, dwu_out, dwd_out,
    gu, hg, ab, hid, go, tok, gos, dw, dws, wg, wu, part, r1, s1, r2, r3, q1, r4,
    gt, rg, tokt, og, ou, od, ot, ss, rs, ls,
):
    z = lax.axis_index("gx")
    gy = lax.axis_index("gy")
    gz = lax.axis_index("gz")
    x, l = gy // 2, gy % 2
    h, c = gz // 2, gz % 2
    nc, nh = 1 - c, 1 - h
    other_gy = x * 2 + (1 - l)
    zs = [lax.rem(z + d, 4) for d in range(4)]

    def zdev(d):
        return (zs[d], gy, gz)

    hidev = (z, gy, nh * 2 + c)
    sib = (z, gy, h * 2 + nc)

    def gydev(dx, dl):
        return (z, lax.rem(x + dx, 4) * 2 + lax.rem(l + dl, 2), gz)

    gy_offsets = [(dx, dl) for dx in range(4) for dl in range(2)][1:]

    sent = []

    def send(src, dst, dev):
        i = len(sent)
        copy = pltpu.make_async_remote_copy(
            src_ref=src, dst_ref=dst, send_sem=ss.at[i], recv_sem=rs.at[i],
            device_id=dev, device_id_type=MESH,
        )
        copy.start()
        sent.append(copy)
        return copy

    def same(ref, dev):
        return send(ref, ref, dev)

    n_local = [0]

    def local(src, dst):
        copy = pltpu.make_async_copy(src, dst, ls.at[n_local[0]])
        n_local[0] += 1
        copy.start()
        return copy

    l_go = local(go_in, go.at[:, :, gy])
    l_gate = local(gate_in, gu.at[0, c, :, z, h])
    l_up = local(up_in, gu.at[1, c, :, z, h])
    l_dw = local(dw_in, dw)
    l_tok = local(tok_in, tok.at[:, :, gy])
    l_wg = local(wg_in, wg)
    l_wu = local(wu_in, wu)

    peers = [sib, hidev] + [zdev(d) for d in (1, 2, 3)] + [gydev(*o) for o in gy_offsets]
    barrier = pltpu.get_barrier_semaphore()
    for dev in peers:
        pl.semaphore_signal(barrier, inc=1, device_id=dev, device_id_type=MESH)
    pl.semaphore_wait(barrier, len(peers))

    l_go.wait()
    go_lo = same(go.at[:, :, gy], gydev(0, 1))
    go_x = [same(go.at[:, :, gy], gydev(d, 0)) for d in (1, 2, 3)]
    l_dw.wait()
    c_dws = send(dw, dws, sib)
    l_gate.wait()
    l_up.wait()
    gu0_hi = same(gu.at[:, c, 0, z, h], hidev)
    gu1_z = [same(gu.at[:, c, 1, z, h], zdev(d)) for d in (1, 2, 3)]
    gu1_hi = [same(gu.at[:, c, 1, z, h], hidev)]

    go_lo.wait_recv()
    go_x2 = [same(go.at[:, :, other_gy], gydev(d, 0)) for d in (1, 2, 3)]
    gu0_hi.wait_recv()
    gu0_z = [same(gu.at[:, c, 0, z], zdev(d)) for d in (1, 2, 3)]

    for copy in go_x + go_x2:
        copy.wait_recv()
    gos_k = [send(go.at[nc, k], gos.at[k], sib) for k in (0, 1)]
    l_tok.wait()
    tok_lo = same(tok.at[:, :, gy], gydev(0, 1))
    tok_x = [same(tok.at[:, :, gy], gydev(d, 0)) for d in (1, 2, 3)]
    c_dws.wait_recv()

    def product(k):
        gos_k[k].wait_recv()
        own = go[c, k].reshape(256, DB)
        other = gos[k].reshape(256, DB)
        for a, b in LANES:
            p = nt(own, dw[a:b, :]) + nt(other, dws[a:b, :])
            part[k, :, :, :, a:b] = p.astype(BF16).reshape(4, 2, 32, b - a)

    product(0)
    rs0_z = [send(part.at[0, zs[d]], r1.at[d - 1], zdev(d)) for d in (1, 2, 3)]
    product(1)
    rs1_hi = send(part.at[1, :, nh], r3, hidev)

    for d in (1, 2, 3):
        gu1_z[d - 1].wait_recv()
        gu1_hi.append(same(gu.at[:, c, 1, zs[4 - d], h], hidev))
    gu1_s = same(gu.at[:, c, 1, :, h], sib)
    tok_lo.wait_recv()
    tok_x2 = [same(tok.at[:, :, other_gy], gydev(d, 0)) for d in (1, 2, 3)]

    rs1_hi.wait_recv()
    for i in range(4):
        for a, b in LANES:
            q1[i, :, a:b] = (part[1, i, h, :, a:b].astype(F32) + r3[i, :, a:b].astype(F32)).astype(BF16)
    rs1_z = [send(q1.at[zs[d]], r4.at[d - 1], zdev(d)) for d in (1, 2, 3)]

    for copy in rs0_z:
        copy.wait_recv()
    for i in range(2):
        for a, b in LANES:
            total = part[0, z, i, :, a:b].astype(F32)
            for d in range(3):
                total = total + r1[d, i, :, a:b].astype(F32)
            s1[i, :, a:b] = total.astype(BF16)
    rs0_hi = send(s1.at[nh], r2, hidev)

    def pointwise(cc, k):
        def block(i, carry):
            zz, hh = i // 2, i % 2
            for a, b in LANES:
                gate = gu[0, cc, k, zz, hh, :, a:b].astype(F32)
                up = gu[1, cc, k, zz, hh, :, a:b].astype(F32)
                s = 0.5 + 0.5 * jnp.tanh(0.5 * gate)
                silu = gate * s
                ab[0, cc, k, zz, hh, :, a:b] = (up * (s * (1.0 + gate - silu))).astype(BF16)
                ab[1, cc, k, zz, hh, :, a:b] = silu.astype(BF16)
                hid[cc, k, zz, hh, :, a:b] = (silu * up).astype(BF16)
            return carry

        lax.fori_loop(0, 8, block, 0)

    for copy in gu0_z:
        copy.wait_recv()
    gu0_s = same(gu.at[:, c, 0], sib)
    pointwise(c, 0)

    for copy in rs1_z:
        copy.wait_recv()
    for a, b in LANES:
        total = q1[z, :, a:b].astype(F32)
        for d in range(3):
            total = total + r4[d, :, a:b].astype(F32)
        hg[c, 1, z, h, :, a:b] = total.astype(BF16)
    hg1_z = [same(hg.at[c, 1, z, h], zdev(d)) for d in (1, 2, 3)]
    hg1_hi = [same(hg.at[c, 1, z, h], hidev)]

    rs0_hi.wait_recv()
    for a, b in LANES:
        total = s1[h, :, a:b].astype(F32) + r2[:, a:b].astype(F32)
        hg[c, 0, z, h, :, a:b] = total.astype(BF16)
    hg0_hi = same(hg.at[c, 0, z, h], hidev)

    for copy in gu1_hi:
        copy.wait_recv()
    gu1_s2 = same(gu.at[:, c, 1, :, nh], sib)
    pointwise(c, 1)

    hg0_hi.wait_recv()
    hg0_z = [same(hg.at[c, 0, z], zdev(d)) for d in (1, 2, 3)]
    hg0_s = [same(hg.at[c, 0, z], sib)]
    for d in (1, 2, 3):
        hg1_z[d - 1].wait_recv()
        hg1_hi.append(same(hg.at[c, 1, zs[4 - d], h], hidev))
    hg1_s = [same(hg.at[c, 1, :, h], sib)]

    gu0_s.wait_recv()
    pointwise(nc, 0)
    gu1_s.wait_recv()
    gu1_s2.wait_recv()
    pointwise(nc, 1)

    stores = []
    for a, b in LANES:
        w = tn(hid[:, :, :, :, :, a:b].reshape(1024, b - a), go[...].reshape(1024, DB))
        od[a:b, :] = (w * SCALE).astype(BF16)
    stores.append(local(od, dwd_out))

    for copy in tok_x + tok_x2:
        copy.wait_recv()
    for cc in range(2):
        for k in range(2):
            i = (cc * 2 + k) * 256
            tokt[:, i : i + 256] = tok[cc, k].reshape(256, DB).T

    l_wg.wait()
    l_wu.wait()

    def input_grad(cc, k):
        def block(i, carry):
            zz, hh = i // 2, i % 2
            for a, b in LANES:
                grad = hg[cc, k, zz, hh, :, a:b]
                ab[0, cc, k, zz, hh, :, a:b] = ab[0, cc, k, zz, hh, :, a:b] * grad
                ab[1, cc, k, zz, hh, :, a:b] = ab[1, cc, k, zz, hh, :, a:b] * grad
            return carry

        lax.fori_loop(0, 8, block, 0)
        term = nt(ab[0, cc, k].reshape(256, FB), wg[...]) + nt(ab[1, cc, k].reshape(256, FB), wu[...])
        gt[cc, k] = term.astype(BF16).reshape(8, 32, DB)

    def send_input_grad(k):
        return [
            send(gt.at[:, k, lax.rem(x + dx, 4) * 2 + lax.rem(l + dl, 2)], rg.at[k, j], gydev(dx, dl))
            for j, (dx, dl) in enumerate(gy_offsets)
        ]

    for d in (1, 2, 3):
        hg0_z[d - 1].wait_recv()
        hg0_s.append(same(hg.at[c, 0, zs[4 - d]], sib))
    input_grad(c, 0)
    for copy in hg0_s:
        copy.wait_recv()
    input_grad(nc, 0)
    gt0 = send_input_grad(0)

    for copy in hg1_hi:
        copy.wait_recv()
    hg1_s.append(same(hg.at[c, 1, :, nh], sib))
    input_grad(c, 1)
    for copy in hg1_s:
        copy.wait_recv()
    input_grad(nc, 1)
    gt1 = send_input_grad(1)

    for which, (out, dst) in enumerate(((og, dwg_out), (ou, dwu_out))):
        for a, b in LANES:
            grads = ab[which, :, :, :, :, :, a:b].reshape(1024, b - a)
            w = jnp.dot(tokt[...], grads, preferred_element_type=F32)
            out[:, a:b] = (w * SCALE).astype(BF16)
        stores.append(local(out, dst))

    for k, copies in enumerate((gt0, gt1)):
        for copy in copies:
            copy.wait_recv()
        for cc in range(2):
            total = gt[cc, k, gy].astype(F32)
            for j in range(7):
                total = total + rg[k, j, cc].astype(F32)
            ot[cc, k] = total.astype(BF16)
    stores.append(local(ot, gt_out))

    for copy in sent:
        copy.wait_send()
    for copy in stores:
        copy.wait()
    assert len(sent) <= N_REMOTE


def local_step(tokens, grad_out, gate_pre, up_pre, gate_weight, up_weight, down_weight):
    any_spec = pl.BlockSpec(memory_space=pl.ANY)
    vm = pltpu.VMEM
    outs = pl.pallas_call(
        kernel,
        out_shape=(
            jax.ShapeDtypeStruct((2, 2, 32, DB), BF16),
            jax.ShapeDtypeStruct((DB, FB), BF16),
            jax.ShapeDtypeStruct((DB, FB), BF16),
            jax.ShapeDtypeStruct((FB, DB), BF16),
        ),
        in_specs=[any_spec] * 7,
        out_specs=(any_spec,) * 4,
        scratch_shapes=[
            vm((2, 2, 2, 4, 2, 32, FB), BF16),
            vm((2, 2, 4, 2, 32, FB), BF16),
            vm((2, 2, 2, 4, 2, 32, FB), BF16),
            vm((2, 2, 4, 2, 32, FB), BF16),
            vm((2, 2, 8, 32, DB), BF16),
            vm((2, 2, 8, 32, DB), BF16),
            vm((2, 8, 32, DB), BF16),
            vm((FB, DB), BF16),
            vm((FB, DB), BF16),
            vm((DB, FB), BF16),
            vm((DB, FB), BF16),
            vm((2, 4, 2, 32, FB), BF16),
            vm((3, 2, 32, FB), BF16),
            vm((2, 32, FB), BF16),
            vm((32, FB), BF16),
            vm((4, 32, FB), BF16),
            vm((4, 32, FB), BF16),
            vm((3, 32, FB), BF16),
            vm((2, 2, 8, 32, DB), BF16),
            vm((2, 7, 2, 32, DB), BF16),
            vm((DB, 1024), BF16),
            vm((DB, FB), BF16),
            vm((DB, FB), BF16),
            vm((FB, DB), BF16),
            vm((2, 2, 32, DB), BF16),
            pltpu.SemaphoreType.DMA((N_REMOTE,)),
            pltpu.SemaphoreType.DMA((N_REMOTE,)),
            pltpu.SemaphoreType.DMA((16,)),
        ],
        compiler_params=pltpu.CompilerParams(
            collective_id=0, has_side_effects=True, vmem_limit_bytes=60 * 1024 * 1024
        ),
        name="swiglu_backward",
    )(
        tokens.reshape(2, 2, 32, DB),
        grad_out.reshape(2, 2, 32, DB),
        gate_pre.reshape(2, 32, FB),
        up_pre.reshape(2, 32, FB),
        gate_weight,
        up_weight,
        down_weight,
    )
    return (outs[0].reshape(128, DB), outs[1], outs[2], outs[3])


def solution(mesh):
    return jax.shard_map(
        local_step,
        mesh=mesh,
        in_specs=(
            P("gy", ("gx", "gz")),
            P("gy", ("gx", "gz")),
            P(("gx", "gz"), "gy"),
            P(("gx", "gz"), "gy"),
            P(("gx", "gz"), "gy"),
            P(("gx", "gz"), "gy"),
            P("gy", ("gx", "gz")),
        ),
        out_specs=(
            P("gy", ("gx", "gz")),
            P(("gx", "gz"), "gy"),
            P(("gx", "gz"), "gy"),
            P("gy", ("gx", "gz")),
        ),
        check_vma=False,
    )
```

```python
import functools
import math

import jax
import jax.numpy as jnp
from jax import lax
from jax.experimental import pallas as pl
from jax.experimental.pallas import tpu as pltpu
from jax.sharding import PartitionSpec as P

MESH = pl.DeviceIdType.MESH
F32 = jnp.float32
BF16 = jnp.bfloat16
FB = 1848
DB = 512
LANES = ((0, 512), (512, 1024), (1024, 1536), (1536, 1848))
N_REMOTE = 112
CHIPS = ((1, 0), (3, 0), (0, 1), (2, 0), (1, 1), (3, 1), (2, 1))
ORDER = ((0, "y"), (1, "z"), (3, "y"), (2, "z"))
SCALE = 1.0 / 32.0


def nt(a, b):
    return lax.dot_general(a, b, (((1,), (1,)), ((), ())), preferred_element_type=F32)


def nn(a, b):
    return lax.dot_general(a, b, (((1,), (0,)), ((), ())), preferred_element_type=F32)


def tn(a, b):
    return lax.dot_general(a, b, (((0,), (0,)), ((), ())), preferred_element_type=F32)


def kernel(
    tok_in, go_in, gate_in, up_in, wg_in, wu_in, dw_in,
    ot, dwg_out, ou, dwd_out,
    gu, hg, ab, hid, go, tok, gos, dw, dws, wg, wu, part, r1, s1, r2, r3, q1, r4, r5,
    gt, rgx, rgd, sl, rl, og, od, ss, rs, ls,
):
    z = lax.axis_index("gx")
    gy = lax.axis_index("gy")
    gz = lax.axis_index("gz")
    x, l = gy // 2, gy % 2
    h, c = gz // 2, gz % 2
    nc, nh = 1 - c, 1 - h
    other_gy = x * 2 + (1 - l)
    zs = [lax.rem(z + d, 4) for d in range(4)]

    def zdev(d):
        return (zs[d], gy, gz)

    hidev = (z, gy, nh * 2 + c)
    sib = (z, gy, h * 2 + nc)

    def chip(e, f):
        return (zs[e], gy, (nh if f else h) * 2 + c)

    def gydev(dx, dl):
        return (z, lax.rem(x + dx, 4) * 2 + lax.rem(l + dl, 2), gz)

    gy_offsets = [(dx, dl) for dx in range(4) for dl in range(2)][1:]

    sent = []

    def remote(src, dst, dev, i):
        return pltpu.make_async_remote_copy(
            src_ref=src, dst_ref=dst, send_sem=ss.at[i], recv_sem=rs.at[i],
            device_id=dev, device_id_type=MESH,
        )

    def send(src, dst, dev):
        copy = remote(src, dst, dev, len(sent))
        copy.start()
        sent.append(copy)
        return copy

    def same(ref, dev):
        return send(ref, ref, dev)

    n_local = [0]

    def local(src, dst):
        copy = pltpu.make_async_copy(src, dst, ls.at[n_local[0]])
        n_local[0] += 1
        copy.start()
        return copy

    l_go = local(go_in, go.at[:, :, gy])
    l_gate = local(gate_in, gu.at[0, c, :, z, h])
    l_up = local(up_in, gu.at[1, c, :, z, h])
    l_dw = local(dw_in, dw)
    l_tok = local(tok_in, tok.at[:, :, gy])
    l_wg = local(wg_in, wg)
    l_wu = local(wu_in, wu)

    peers = [sib, hidev] + [zdev(d) for d in (1, 2, 3)] + [gydev(*o) for o in gy_offsets]
    barrier = pltpu.get_barrier_semaphore()
    for dev in peers:
        pl.semaphore_signal(barrier, inc=1, device_id=dev, device_id_type=MESH)
    pl.semaphore_wait(barrier, len(peers))

    l_go.wait()
    go_lo = same(go.at[:, :, gy], gydev(0, 1))
    go_own = {d: same(go.at[:, :, gy], gydev(d, 0)) for d in (1, 3, 2)}
    l_dw.wait()
    c_dws = send(dw, dws, sib)
    l_gate.wait()
    l_up.wait()
    gu1_z = [same(gu.at[:, c, 1, z, h], zdev(d)) for d in (1, 3)]
    gu0_hi = same(gu.at[:, c, 0, z, h], hidev)
    gu1_hi = [same(gu.at[:, c, 1, z, h], hidev)]
    go_lo.wait_recv()
    go_other = {d: same(go.at[:, :, other_gy], gydev(d, 0)) for d in (1, 3, 2)}

    xts = {d: lax.rem(x + (4 - d), 4) for d in range(4)}
    kind = dict(ORDER)
    slot = {d: [e for e, t in ORDER if t == kind[d]].index(d) for d in kind}
    zk, zh = [v // 2 for v in zs], [v % 2 for v in zs]
    mine = pl.ds(pl.multiple_of(h * 16, 16), 16)
    theirs = pl.ds(pl.multiple_of(nh * 16, 16), 16)
    one, two, spread_one, spread_two, to_sib, gt_copies, gt_last = {}, {}, {}, {}, {}, [], []

    def product(d):
        xt = xts[d]
        pair = pl.ds(xt * 2, 2)
        if d:
            go_own[d].wait_recv()
            go_other[d].wait_recv()
        gos_d = send(go.at[nc, :, pair], gos.at[:, pair], sib)
        if not d:
            c_dws.wait_recv()
        gos_d.wait_recv()
        own = go[c, :, pair].reshape(128, DB)
        other = gos[:, pair].reshape(128, DB)
        for a, b in LANES:
            p = nt(own, dw[a:b, :]) + nt(other, dws[a:b, :])
            part[xt, :, :, :, a:b] = p.astype(BF16).reshape(2, 2, 32, b - a)
        if kind[d] == "z":
            one[d] = [send(part.at[xt, zk[e], zh[e]], r1.at[slot[d], e - 1], zdev(e)) for e in (1, 3, 2)]
        elif kind[d] == "d":
            one[d] = [
                send(part.at[xt, zk[e], zh[e], (mine, theirs)[f]], r5.at[slot[d], j], chip(e, f))
                for j, (e, f) in enumerate(CHIPS)
            ]
        else:
            one[d] = [send(part.at[xt, :, :, theirs], r3.at[slot[d]], hidev)]

    def middle(d):
        xt, i = xts[d], slot[d]
        if kind[d] == "d":
            return
        for copy in one[d]:
            copy.wait_recv()
        if kind[d] == "z":
            for a, b in LANES:
                total = part[xt, zk[0], zh[0], :, a:b].astype(F32)
                for e in range(3):
                    total = total + r1[i, e, :, a:b].astype(F32)
                s1[i, :, a:b] = total.astype(BF16)
            two[d] = [send(s1.at[i, theirs], r2.at[i], hidev)]
        else:
            for a, b in LANES:
                total = part[xt, :, :, mine, a:b].astype(F32) + r3[i, :, :, :, a:b].astype(F32)
                q1[i, :, :, :, a:b] = total.astype(BF16)
            two[d] = [send(q1.at[i, zk[e], zh[e]], r4.at[i, e - 1], zdev(e)) for e in (1, 3, 2)]

    def own_sum(d):
        xt, i = xts[d], slot[d]
        for copy in one[d] if kind[d] == "d" else two[d]:
            copy.wait_recv()
        for a, b in LANES:
            if kind[d] == "z":
                total = s1[i, mine, a:b].astype(F32) + r2[i, :, a:b].astype(F32)
            elif kind[d] == "d":
                total = part[xt, zk[0], zh[0], mine, a:b].astype(F32)
                for j in range(7):
                    total = total + r5[i, j, :, a:b].astype(F32)
            else:
                total = q1[i, zk[0], zh[0], :, a:b].astype(F32)
                for e in range(3):
                    total = total + r4[i, e, :, a:b].astype(F32)
            hg[c, zk[0], xt, zh[0], mine, a:b] = total.astype(BF16)
        block = hg.at[c, zk[0], xt, zh[0], mine]
        if kind[d] == "z":
            spread_one[d] = [same(block, hidev)]
        elif kind[d] == "d":
            spread_one[d] = [same(block, chip(e, f)) for e, f in CHIPS]
        else:
            spread_one[d] = [same(block, zdev(e)) for e in (1, 2, 3)]
            spread_two[d] = [same(block, hidev)]

    def spread(d):
        xt = xts[d]
        if kind[d] == "d":
            return
        if kind[d] == "z":
            spread_one[d][0].wait_recv()
            pair = hg.at[c, zk[0], xt, zh[0]]
            spread_two[d] = [same(pair, zdev(e)) for e in (1, 2, 3)]
            to_sib[d] = [same(pair, sib)]
        else:
            for e in (1, 2, 3):
                spread_one[d][e - 1].wait_recv()
                spread_two[d].append(same(hg.at[c, zk[4 - e], xt, zh[4 - e], mine], hidev))
            to_sib[d] = [same(hg.at[c, :, xt, :, mine], sib)]

    def last_spread(d):
        xt = xts[d]
        if kind[d] == "z":
            for e in (1, 2, 3):
                spread_two[d][e - 1].wait_recv()
                to_sib[d].append(same(hg.at[c, zk[4 - e], xt, zh[4 - e]], sib))
        elif kind[d] == "d":
            for copy in spread_one[d]:
                copy.wait_recv()
            to_sib[d] = [same(hg.at[c, :, xt], sib)]
        else:
            for copy in spread_two[d]:
                copy.wait_recv()
            to_sib[d].append(same(hg.at[c, :, xt, :, theirs], sib))

    def input_grad(d):
        xt = xts[d]
        for copy in to_sib[d]:
            copy.wait_recv()

        def block(i, carry):
            cc, k, hh = i // 4, (i // 2) % 2, i % 2
            for a, b in LANES:
                grad = hg[cc, k, xt, hh, :, a:b]
                ab[0, cc, k, xt, hh, :, a:b] = ab[0, cc, k, xt, hh, :, a:b] * grad
                ab[1, cc, k, xt, hh, :, a:b] = ab[1, cc, k, xt, hh, :, a:b] * grad
            return carry

        lax.fori_loop(0, 8, block, 0)
        term = nn(ab[0, :, :, xt].reshape(256, FB), wg[...])
        term = term + nn(ab[1, :, :, xt].reshape(256, FB), wu[...])
        term = term.astype(BF16).reshape(2, 2, 2, 32, DB)
        for hh in range(2):
            gt[xt, hh] = term[:, :, hh]
        if d == ORDER[-1][0]:
            gt_last.append(send(gt.at[xt, l], rgd.at[0], (z, xt * 2 + l, gz)))
            gt_last.append(send(gt.at[xt, 1 - l], rgd.at[1], (z, xt * 2 + 1 - l, gz)))
        elif d:
            gt_copies.append(send(gt.at[xt], rgx.at[len(gt_copies)], (z, xt * 2 + l, gz)))

    def pointwise(cc, k):
        def block(i, carry):
            zz, hh = i // 2, i % 2
            for a, b in LANES:
                gate = gu[0, cc, k, zz, hh, :, a:b].astype(F32)
                up = gu[1, cc, k, zz, hh, :, a:b].astype(F32)
                s = 0.5 + 0.5 * jnp.tanh(0.5 * gate)
                silu = gate * s
                ab[0, cc, k, zz, hh, :, a:b] = (up * (s * (1.0 + gate - silu))).astype(BF16)
                ab[1, cc, k, zz, hh, :, a:b] = silu.astype(BF16)
                hid[cc, k, zz, hh, :, a:b] = (silu * up).astype(BF16)
            return carry

        lax.fori_loop(0, 8, block, 0)

    d0, d1, d2, d3 = [d for d, _ in ORDER]
    product(d0)
    gu1_z[0].wait_recv()
    gu1_f = [same(gu.at[0, c, 1, zs[3], h], zdev(1))]
    gu1_z[1].wait_recv()
    gu1_f.append(same(gu.at[1, c, 1, zs[1], h], zdev(3)))
    gu0_hi.wait_recv()
    gu0_z = [same(gu.at[:, c, 0, z], zdev(d)) for d in (1, 3)]
    product(d1)
    gu1_hi += [same(gu.at[:, c, 1, zs[d], h], hidev) for d in (1, 3)]
    product(d2)
    middle(d0)
    product(d3)
    middle(d1)
    l_tok.wait()
    tok_lo = same(tok.at[:, :, gy], gydev(0, 1))
    tok_x = [same(tok.at[:, :, gy], gydev(d, 0)) for d in (1, 2, 3)]
    own_sum(d0)
    middle(d2)
    for copy in gu1_f:
        copy.wait_recv()
    gu1_hi.append(same(gu.at[:, c, 1, zs[2], h], hidev))
    gu1_s = same(gu.at[:, c, 1, :, h], sib)
    own_sum(d1)
    spread(d0)
    middle(d3)
    gu0_z[0].wait_recv()
    gu0_f = [same(gu.at[0, c, 0, zs[3]], zdev(1))]
    gu0_z[1].wait_recv()
    gu0_f.append(same(gu.at[1, c, 0, zs[1]], zdev(3)))
    own_sum(d2)
    spread(d1)
    tok_lo.wait_recv()
    tok_x2 = [same(tok.at[:, :, other_gy], gydev(d, 0)) for d in (1, 2, 3)]
    last_spread(d0)
    own_sum(d3)
    spread(d2)
    for copy in gu1_hi:
        copy.wait_recv()
    gu1_s2 = same(gu.at[:, c, 1, :, nh], sib)
    pointwise(c, 1)
    last_spread(d1)
    spread(d3)
    for copy in gu0_f:
        copy.wait_recv()
    gu0_s = same(gu.at[:, c, 0], sib)
    pointwise(c, 0)
    gu1_s.wait_recv()
    gu1_s2.wait_recv()
    pointwise(nc, 1)
    last_spread(d2)
    gu0_s.wait_recv()
    pointwise(nc, 0)
    l_wg.wait()
    l_wu.wait()
    input_grad(d0)
    last_spread(d3)
    input_grad(d1)
    input_grad(d2)
    input_grad(d3)
    for copy in gt_copies:
        copy.wait_recv()
    for cc in range(2):
        total = gt[x, 1 - l, cc].astype(F32) + rgx[0, 1 - l, cc].astype(F32) + rgx[1, 1 - l, cc].astype(F32)
        sl[cc] = total.astype(BF16)
    gt_last.append(send(sl, rl, gydev(0, 1)))
    for copy in tok_x + tok_x2:
        copy.wait_recv()
    stores = []
    for a, b in LANES:
        w = tn(hid[:, :, :, :, :, a:b].reshape(1024, b - a), go[...].reshape(1024, DB))
        od[a:b, :] = (w * SCALE).astype(BF16)
    stores.append(local(od, dwd_out))
    for which, out in enumerate((og, ou)):
        for a, b in LANES:
            grads = ab[which, :, :, :, :, :, a:b].reshape(1024, b - a)
            w = tn(grads, tok[...].reshape(1024, DB))
            out[a:b, :] = (w * SCALE).astype(BF16)
        if which == 0:
            stores.append(local(og, dwg_out))

    for copy in gt_last:
        copy.wait_recv()
    for cc in range(2):
        total = gt[x, l, cc].astype(F32) + rl[cc].astype(F32)
        for j in range(2):
            total = total + rgx[j, l, cc].astype(F32) + rgd[j, cc].astype(F32)
        ot[cc] = total.astype(BF16)
    for copy in sent:
        copy.wait_send()
    for copy in stores:
        copy.wait()
    assert len(sent) <= N_REMOTE


def copy_kernel(gt_in, dwg_in, dwu_in, dwd_in, gt_out, dwg_out, dwu_out, dwd_out, held_g, held_d, sems):
    reads = [
        pltpu.make_async_copy(dwg_in, held_g, sems.at[0]),
        pltpu.make_async_copy(dwd_in, held_d, sems.at[1]),
    ]
    writes = [
        pltpu.make_async_copy(held_g, dwg_out, sems.at[2]),
        pltpu.make_async_copy(held_d, dwd_out, sems.at[3]),
        pltpu.make_async_copy(gt_in, gt_out, sems.at[4]),
        pltpu.make_async_copy(dwu_in, dwu_out, sems.at[5]),
    ]
    for copy in reads + writes[2:]:
        copy.start()
    for read, write in zip(reads, writes):
        read.wait()
        write.start()
    for copy in writes:
        copy.wait()


def local_step(tokens, grad_out, gate_pre, up_pre, gate_weight, up_weight, down_weight):
    any_spec = pl.BlockSpec(memory_space=pl.ANY)
    vm = pltpu.VMEM
    vm_spec = pl.BlockSpec(memory_space=vm)
    outs = pl.pallas_call(
        kernel,
        out_shape=(
            vm((2, 2, 32, DB), BF16),
            jax.ShapeDtypeStruct((FB, DB), BF16),
            vm((FB, DB), BF16),
            jax.ShapeDtypeStruct((FB, DB), BF16),
        ),
        in_specs=[any_spec] * 7,
        out_specs=(vm_spec, any_spec, vm_spec, any_spec),
        scratch_shapes=[
            vm((2, 2, 2, 4, 2, 32, FB), BF16),
            vm((2, 2, 4, 2, 32, FB), BF16),
            vm((2, 2, 2, 4, 2, 32, FB), BF16),
            vm((2, 2, 4, 2, 32, FB), BF16),
            vm((2, 2, 8, 32, DB), BF16),
            vm((2, 2, 8, 32, DB), BF16),
            vm((2, 8, 32, DB), BF16),
            vm((FB, DB), BF16),
            vm((FB, DB), BF16),
            vm((FB, DB), BF16),
            vm((FB, DB), BF16),
            vm((4, 2, 2, 32, FB), BF16),
            vm((4, 3, 32, FB), BF16),
            vm((4, 32, FB), BF16),
            vm((4, 16, FB), BF16),
            vm((4, 2, 2, 16, FB), BF16),
            vm((4, 2, 2, 16, FB), BF16),
            vm((4, 3, 16, FB), BF16),
            vm((4, 7, 16, FB), BF16),
            vm((4, 2, 2, 2, 32, DB), BF16),
            vm((2, 2, 2, 2, 32, DB), BF16),
            vm((2, 2, 2, 32, DB), BF16),
            vm((2, 2, 32, DB), BF16),
            vm((2, 2, 32, DB), BF16),
            vm((FB, DB), BF16),
            vm((FB, DB), BF16),
            pltpu.SemaphoreType.DMA((N_REMOTE,)),
            pltpu.SemaphoreType.DMA((N_REMOTE,)),
            pltpu.SemaphoreType.DMA((16,)),
        ],
        compiler_params=pltpu.CompilerParams(
            collective_id=0, has_side_effects=True, vmem_limit_bytes=60 * 1024 * 1024
        ),
        name="swiglu_backward",
    )(
        tokens.reshape(2, 2, 32, DB),
        grad_out.reshape(2, 2, 32, DB),
        gate_pre.reshape(2, 32, FB),
        up_pre.reshape(2, 32, FB),
        gate_weight.T,
        up_weight.T,
        down_weight,
    )
    outs = pl.pallas_call(
        copy_kernel,
        out_shape=tuple(jax.ShapeDtypeStruct(o.shape, o.dtype) for o in outs),
        in_specs=[vm_spec, any_spec, vm_spec, any_spec],
        out_specs=(any_spec,) * 4,
        scratch_shapes=[vm((FB, DB), BF16)] * 2 + [pltpu.SemaphoreType.DMA((6,))],
        name="hand_out",
    )(
        pltpu.with_memory_space_constraint(outs[0], vm),
        outs[1],
        pltpu.with_memory_space_constraint(outs[2], vm),
        outs[3],
    )
    return (outs[0].reshape(128, DB), outs[1].T, outs[2].T, outs[3])


def solution(mesh):
    return jax.shard_map(
        local_step,
        mesh=mesh,
        in_specs=(
            P("gy", ("gx", "gz")),
            P("gy", ("gx", "gz")),
            P(("gx", "gz"), "gy"),
            P(("gx", "gz"), "gy"),
            P(("gx", "gz"), "gy"),
            P(("gx", "gz"), "gy"),
            P("gy", ("gx", "gz")),
        ),
        out_specs=(
            P("gy", ("gx", "gz")),
            P(("gx", "gz"), "gy"),
            P(("gx", "gz"), "gy"),
            P("gy", ("gx", "gz")),
        ),
        check_vma=False,
    )
```

```python
import functools
import math

import jax
import jax.numpy as jnp
from jax import lax
from jax.experimental import pallas as pl
from jax.experimental.pallas import tpu as pltpu
from jax.sharding import PartitionSpec as P

MESH = pl.DeviceIdType.MESH
F32 = jnp.float32
BF16 = jnp.bfloat16
FB = 1848
DB = 512
LANES = ((0, 512), (512, 1024), (1024, 1536), (1536, 1848))
N_REMOTE = 112
ORDER = ((1, "y"), (0, "z"), (3, "z"), (2, "y"))
SCALE = 1.0 / 32.0


def nt(a, b):
    return lax.dot_general(a, b, (((1,), (1,)), ((), ())), preferred_element_type=F32)


def nn(a, b):
    return lax.dot_general(a, b, (((1,), (0,)), ((), ())), preferred_element_type=F32)


def tn(a, b):
    return lax.dot_general(a, b, (((0,), (0,)), ((), ())), preferred_element_type=F32)


def kernel(
    tok_in, go_in, gate_in, up_in, wg_in, wu_in, dw_in,
    ot, dwg_out, ou, dwd_out,
    gu, hg, ab, hid, go, tok, gos, dw, dws, wg, wu, part, r1, s1, r2, r3, q1, r4,
    gt, rgx, rgd, sl, rl, og, od, ss, rs, ls,
):
    z = lax.axis_index("gx")
    gy = lax.axis_index("gy")
    gz = lax.axis_index("gz")
    x, l = gy // 2, gy % 2
    h, c = gz // 2, gz % 2
    nc, nh = 1 - c, 1 - h
    other_gy = x * 2 + (1 - l)
    zs = [lax.rem(z + d, 4) for d in range(4)]

    def zdev(d):
        return (zs[d], gy, gz)

    hidev = (z, gy, nh * 2 + c)
    sib = (z, gy, h * 2 + nc)

    def gydev(dx, dl):
        return (z, lax.rem(x + dx, 4) * 2 + lax.rem(l + dl, 2), gz)

    gy_offsets = [(dx, dl) for dx in range(4) for dl in range(2)][1:]

    sent = []

    def remote(src, dst, dev, i):
        return pltpu.make_async_remote_copy(
            src_ref=src, dst_ref=dst, send_sem=ss.at[i], recv_sem=rs.at[i],
            device_id=dev, device_id_type=MESH,
        )

    def send(src, dst, dev):
        copy = remote(src, dst, dev, len(sent))
        copy.start()
        sent.append(copy)
        return copy

    def same(ref, dev):
        return send(ref, ref, dev)

    n_local = [0]

    def local(src, dst):
        copy = pltpu.make_async_copy(src, dst, ls.at[n_local[0]])
        n_local[0] += 1
        copy.start()
        return copy

    l_go = local(go_in, go.at[:, :, gy])
    l_gate = local(gate_in, gu.at[0, c, :, z, h])
    l_up = local(up_in, gu.at[1, c, :, z, h])
    l_dw = local(dw_in, dw)
    l_tok = local(tok_in, tok.at[:, :, gy])
    l_wg = local(wg_in, wg)
    l_wu = local(wu_in, wu)

    peers = [sib, hidev] + [zdev(d) for d in (1, 2, 3)] + [gydev(*o) for o in gy_offsets]
    barrier = pltpu.get_barrier_semaphore()
    for dev in peers:
        pl.semaphore_signal(barrier, inc=1, device_id=dev, device_id_type=MESH)
    pl.semaphore_wait(barrier, len(peers))

    l_go.wait()
    go_lo = same(go.at[:, :, gy], gydev(0, 1))
    go_own = {d: same(go.at[:, :, gy], gydev(d, 0)) for d in (1, 3, 2)}
    l_dw.wait()
    c_dws = send(dw, dws, sib)
    l_gate.wait()
    l_up.wait()
    gu1_z = [same(gu.at[:, c, 1, z, h], zdev(d)) for d in (1, 3)]
    gu0_hi = same(gu.at[:, c, 0, z, h], hidev)
    gu1_hi = [same(gu.at[:, c, 1, z, h], hidev)]
    go_lo.wait_recv()
    go_other = {d: same(go.at[:, :, other_gy], gydev(d, 0)) for d in (1, 3, 2)}

    xts = {d: lax.rem(x + (4 - d), 4) for d in range(4)}
    kind = dict(ORDER)
    slot = {d: [e for e, t in ORDER if t == kind[d]].index(d) for d in kind}
    zk, zh = [v // 2 for v in zs], [v % 2 for v in zs]
    mine = pl.ds(pl.multiple_of(h * 16, 16), 16)
    theirs = pl.ds(pl.multiple_of(nh * 16, 16), 16)
    one, two, spread_one, spread_two, to_sib, gt_copies, gt_last = {}, {}, {}, {}, {}, [], []

    def product(d):
        xt = xts[d]
        pair = pl.ds(xt * 2, 2)
        if d:
            go_own[d].wait_recv()
            go_other[d].wait_recv()
        gos_d = send(go.at[nc, :, pair], gos.at[:, pair], sib)
        if not d:
            c_dws.wait_recv()
        gos_d.wait_recv()
        own = go[c, :, pair].reshape(128, DB)
        other = gos[:, pair].reshape(128, DB)
        for a, b in LANES:
            p = nt(own, dw[a:b, :]) + nt(other, dws[a:b, :])
            part[xt, :, :, :, a:b] = p.astype(BF16).reshape(2, 2, 32, b - a)
        if kind[d] == "z":
            one[d] = [send(part.at[xt, zk[e], zh[e]], r1.at[slot[d], e - 1], zdev(e)) for e in (1, 3, 2)]
        else:
            one[d] = [send(part.at[xt, :, :, theirs], r3.at[slot[d]], hidev)]

    def middle(d):
        xt, i = xts[d], slot[d]
        for copy in one[d]:
            copy.wait_recv()
        if kind[d] == "z":
            for a, b in LANES:
                total = part[xt, zk[0], zh[0], :, a:b].astype(F32)
                for e in range(3):
                    total = total + r1[i, e, :, a:b].astype(F32)
                s1[i, :, a:b] = total.astype(BF16)
            two[d] = [send(s1.at[i, theirs], r2.at[i], hidev)]
        else:
            for a, b in LANES:
                total = part[xt, :, :, mine, a:b].astype(F32) + r3[i, :, :, :, a:b].astype(F32)
                q1[i, :, :, :, a:b] = total.astype(BF16)
            two[d] = [send(q1.at[i, zk[e], zh[e]], r4.at[i, e - 1], zdev(e)) for e in (1, 3, 2)]

    def own_sum(d):
        xt, i = xts[d], slot[d]
        for copy in two[d]:
            copy.wait_recv()
        for a, b in LANES:
            if kind[d] == "z":
                total = s1[i, mine, a:b].astype(F32) + r2[i, :, a:b].astype(F32)
            else:
                total = q1[i, zk[0], zh[0], :, a:b].astype(F32)
                for e in range(3):
                    total = total + r4[i, e, :, a:b].astype(F32)
            hg[c, zk[0], xt, zh[0], mine, a:b] = total.astype(BF16)
        block = hg.at[c, zk[0], xt, zh[0], mine]
        if kind[d] == "z":
            spread_one[d] = [same(block, hidev)]
        else:
            spread_one[d] = [same(block, zdev(e)) for e in (1, 2, 3)]
            spread_two[d] = [same(block, hidev)]

    def spread(d):
        xt = xts[d]
        if kind[d] == "z":
            spread_one[d][0].wait_recv()
            pair = hg.at[c, zk[0], xt, zh[0]]
            spread_two[d] = [same(pair, zdev(e)) for e in (1, 2, 3)]
            to_sib[d] = [same(pair, sib)]
        else:
            for e in (1, 2, 3):
                spread_one[d][e - 1].wait_recv()
                spread_two[d].append(same(hg.at[c, zk[4 - e], xt, zh[4 - e], mine], hidev))
            to_sib[d] = [same(hg.at[c, :, xt, :, mine], sib)]

    def last_spread(d):
        xt = xts[d]
        if kind[d] == "z":
            for e in (1, 2, 3):
                spread_two[d][e - 1].wait_recv()
                to_sib[d].append(same(hg.at[c, zk[4 - e], xt, zh[4 - e]], sib))
        else:
            for copy in spread_two[d]:
                copy.wait_recv()
            to_sib[d].append(same(hg.at[c, :, xt, :, theirs], sib))

    def input_grad(d):
        xt = xts[d]
        for copy in to_sib[d]:
            copy.wait_recv()

        def block(i, carry):
            cc, k, hh = i // 4, (i // 2) % 2, i % 2
            for a, b in LANES:
                grad = hg[cc, k, xt, hh, :, a:b]
                ab[0, cc, k, xt, hh, :, a:b] = ab[0, cc, k, xt, hh, :, a:b] * grad
                ab[1, cc, k, xt, hh, :, a:b] = ab[1, cc, k, xt, hh, :, a:b] * grad
            return carry

        lax.fori_loop(0, 8, block, 0)
        term = nn(ab[0, :, :, xt].reshape(256, FB), wg[...])
        term = term + nn(ab[1, :, :, xt].reshape(256, FB), wu[...])
        term = term.astype(BF16).reshape(2, 2, 2, 32, DB)
        for hh in range(2):
            gt[xt, hh] = term[:, :, hh]
        if d == ORDER[-1][0]:
            gt_last.append(send(gt.at[xt, l], rgd.at[0], (z, xt * 2 + l, gz)))
            gt_last.append(send(gt.at[xt, 1 - l], rgd.at[1], (z, xt * 2 + 1 - l, gz)))
        elif d:
            gt_copies.append(send(gt.at[xt], rgx.at[len(gt_copies)], (z, xt * 2 + l, gz)))

    def pointwise(cc, k, part_of):
        def block(i, carry):
            zz, hh = i // 2, i % 2
            for a, b in LANES:
                gate = gu[0, cc, k, zz, hh, :, a:b].astype(F32)
                up = gu[1, cc, k, zz, hh, :, a:b].astype(F32)
                s = 0.5 + 0.5 * jnp.tanh(0.5 * gate)
                silu = gate * s
                ab[0, cc, k, zz, hh, :, a:b] = (up * (s * (1.0 + gate - silu))).astype(BF16)
                ab[1, cc, k, zz, hh, :, a:b] = silu.astype(BF16)
                hid[cc, k, zz, hh, :, a:b] = (silu * up).astype(BF16)
            return carry

        lax.fori_loop(4 * part_of, 4 * part_of + 4, block, 0)

    gu1_f, gu0_z, gu0_f, gu_s, tok_lo, tok_x, lo_sum, stores = [], [], [], {}, [], [], [], []

    def gate_up_1():
        gu1_z[0].wait_recv()
        gu1_f.append(same(gu.at[0, c, 1, zs[3], h], zdev(1)))
        gu1_z[1].wait_recv()
        gu1_f.append(same(gu.at[1, c, 1, zs[1], h], zdev(3)))

    def gate_up_2():
        gu0_hi.wait_recv()
        gu0_z.extend([same(gu.at[:, c, 0, z], zdev(d)) for d in (1, 3)])

    def gate_up_3():
        gu1_hi.extend([same(gu.at[:, c, 1, zs[d], h], hidev) for d in (1, 3)])

    def gate_up_4():
        for copy in gu1_f:
            copy.wait_recv()
        gu1_hi.append(same(gu.at[:, c, 1, zs[2], h], hidev))
        gu_s[0] = same(gu.at[:, c, 1, :, h], sib)

    def gate_up_5():
        gu0_z[0].wait_recv()
        gu0_f.append(same(gu.at[0, c, 0, zs[3]], zdev(1)))
        gu0_z[1].wait_recv()
        gu0_f.append(same(gu.at[1, c, 0, zs[1]], zdev(3)))

    def gate_up_6():
        for copy in gu1_hi:
            copy.wait_recv()
        gu_s[1] = same(gu.at[:, c, 1, :, nh], sib)

    def gate_up_7():
        for copy in gu0_f:
            copy.wait_recv()
        gu_s[2] = same(gu.at[:, c, 0], sib)

    def tokens_1():
        l_tok.wait()
        tok_lo.append(same(tok.at[:, :, gy], gydev(0, 1)))
        tok_x.extend([same(tok.at[:, :, gy], gydev(d, 0)) for d in (1, 2, 3)])

    def tokens_2():
        tok_lo[0].wait_recv()
        tok_x.extend([same(tok.at[:, :, other_gy], gydev(d, 0)) for d in (1, 2, 3)])

    def sum_lo():
        for copy in gt_copies:
            copy.wait_recv()
        for cc in range(2):
            total = gt[x, 1 - l, cc].astype(F32) + rgx[0, 1 - l, cc].astype(F32) + rgx[1, 1 - l, cc].astype(F32)
            sl[cc] = total.astype(BF16)
        gt_last.append(send(sl, rl, gydev(0, 1)))

    def down_grad():
        for a, b in LANES:
            w = tn(hid[:, :, :, :, :, a:b].reshape(1024, b - a), go[...].reshape(1024, DB))
            od[a:b, :] = (w * SCALE).astype(BF16)
        stores.append(local(od, dwd_out))

    gate_up_1()
    gate_up_3()
    product(0)
    gate_up_2()
    middle(0)
    product(3)
    gate_up_4()
    gu_s[0].wait_recv()
    product(1)
    product(2)
    gate_up_6()
    gate_up_5()
    middle(3)
    middle(1)
    own_sum(3)
    gu_s[1].wait_recv()
    gate_up_7()
    pointwise(nc, 1, 1)
    middle(2)
    pointwise(c, 1, 0)
    tokens_1()
    pointwise(nc, 1, 0)
    own_sum(1)
    gu_s[2].wait_recv()
    pointwise(c, 0, 1)
    pointwise(c, 0, 0)
    spread(3)
    own_sum(0)
    pointwise(nc, 0, 0)
    spread(1)
    pointwise(nc, 0, 1)
    own_sum(2)
    pointwise(c, 1, 1)
    tokens_2()
    down_grad()
    last_spread(3)
    last_spread(1)
    spread(0)
    spread(2)
    l_wg.wait()
    l_wu.wait()
    input_grad(3)
    input_grad(1)
    last_spread(2)
    last_spread(0)
    input_grad(2)
    input_grad(0)
    sum_lo()
    for copy in tok_x:
        copy.wait_recv()

    for which, out in enumerate((og, ou)):
        for a, b in LANES:
            grads = ab[which, :, :, :, :, :, a:b].reshape(1024, b - a)
            w = tn(grads, tok[...].reshape(1024, DB))
            out[a:b, :] = (w * SCALE).astype(BF16)
        if which == 0:
            stores.append(local(og, dwg_out))

    for copy in gt_last:
        copy.wait_recv()
    for cc in range(2):
        total = gt[x, l, cc].astype(F32) + rl[cc].astype(F32)
        for j in range(2):
            total = total + rgx[j, l, cc].astype(F32) + rgd[j, cc].astype(F32)
        ot[cc] = total.astype(BF16)
    for copy in sent:
        copy.wait_send()
    for copy in stores:
        copy.wait()
    assert len(sent) <= N_REMOTE


def copy_kernel(gt_in, dwg_in, dwu_in, dwd_in, gt_out, dwg_out, dwu_out, dwd_out, held_g, held_d, sems):
    reads = [
        pltpu.make_async_copy(dwg_in, held_g, sems.at[0]),
        pltpu.make_async_copy(dwd_in, held_d, sems.at[1]),
    ]
    writes = [
        pltpu.make_async_copy(held_g, dwg_out, sems.at[2]),
        pltpu.make_async_copy(held_d, dwd_out, sems.at[3]),
        pltpu.make_async_copy(gt_in, gt_out, sems.at[4]),
        pltpu.make_async_copy(dwu_in, dwu_out, sems.at[5]),
    ]
    for copy in reads + writes[2:]:
        copy.start()
    for read, write in zip(reads, writes):
        read.wait()
        write.start()
    for copy in writes:
        copy.wait()


def local_step(tokens, grad_out, gate_pre, up_pre, gate_weight, up_weight, down_weight):
    any_spec = pl.BlockSpec(memory_space=pl.ANY)
    vm = pltpu.VMEM
    vm_spec = pl.BlockSpec(memory_space=vm)
    outs = pl.pallas_call(
        kernel,
        out_shape=(
            vm((2, 2, 32, DB), BF16),
            jax.ShapeDtypeStruct((FB, DB), BF16),
            vm((FB, DB), BF16),
            jax.ShapeDtypeStruct((FB, DB), BF16),
        ),
        in_specs=[any_spec] * 7,
        out_specs=(vm_spec, any_spec, vm_spec, any_spec),
        scratch_shapes=[
            vm((2, 2, 2, 4, 2, 32, FB), BF16),
            vm((2, 2, 4, 2, 32, FB), BF16),
            vm((2, 2, 2, 4, 2, 32, FB), BF16),
            vm((2, 2, 4, 2, 32, FB), BF16),
            vm((2, 2, 8, 32, DB), BF16),
            vm((2, 2, 8, 32, DB), BF16),
            vm((2, 8, 32, DB), BF16),
            vm((FB, DB), BF16),
            vm((FB, DB), BF16),
            vm((FB, DB), BF16),
            vm((FB, DB), BF16),
            vm((4, 2, 2, 32, FB), BF16),
            vm((4, 3, 32, FB), BF16),
            vm((4, 32, FB), BF16),
            vm((4, 16, FB), BF16),
            vm((4, 2, 2, 16, FB), BF16),
            vm((4, 2, 2, 16, FB), BF16),
            vm((4, 3, 16, FB), BF16),
            vm((4, 2, 2, 2, 32, DB), BF16),
            vm((2, 2, 2, 2, 32, DB), BF16),
            vm((2, 2, 2, 32, DB), BF16),
            vm((2, 2, 32, DB), BF16),
            vm((2, 2, 32, DB), BF16),
            vm((FB, DB), BF16),
            vm((FB, DB), BF16),
            pltpu.SemaphoreType.DMA((N_REMOTE,)),
            pltpu.SemaphoreType.DMA((N_REMOTE,)),
            pltpu.SemaphoreType.DMA((16,)),
        ],
        compiler_params=pltpu.CompilerParams(
            collective_id=0, has_side_effects=True, vmem_limit_bytes=60 * 1024 * 1024
        ),
        name="swiglu_backward",
    )(
        tokens.reshape(2, 2, 32, DB),
        grad_out.reshape(2, 2, 32, DB),
        gate_pre.reshape(2, 32, FB),
        up_pre.reshape(2, 32, FB),
        gate_weight.T,
        up_weight.T,
        down_weight,
    )
    outs = pl.pallas_call(
        copy_kernel,
        out_shape=tuple(jax.ShapeDtypeStruct(o.shape, o.dtype) for o in outs),
        in_specs=[vm_spec, any_spec, vm_spec, any_spec],
        out_specs=(any_spec,) * 4,
        scratch_shapes=[vm((FB, DB), BF16)] * 2 + [pltpu.SemaphoreType.DMA((6,))],
        name="hand_out",
    )(
        pltpu.with_memory_space_constraint(outs[0], vm),
        outs[1],
        pltpu.with_memory_space_constraint(outs[2], vm),
        outs[3],
    )
    return (outs[0].reshape(128, DB), outs[1].T, outs[2].T, outs[3])


def solution(mesh):
    return jax.shard_map(
        local_step,
        mesh=mesh,
        in_specs=(
            P("gy", ("gx", "gz")),
            P("gy", ("gx", "gz")),
            P(("gx", "gz"), "gy"),
            P(("gx", "gz"), "gy"),
            P(("gx", "gz"), "gy"),
            P(("gx", "gz"), "gy"),
            P("gy", ("gx", "gz")),
        ),
        out_specs=(
            P("gy", ("gx", "gz")),
            P(("gx", "gz"), "gy"),
            P(("gx", "gz"), "gy"),
            P("gy", ("gx", "gz")),
        ),
        check_vma=False,
    )
```

```python
import functools
import math

import jax
import jax.numpy as jnp
from jax import lax
from jax.experimental import pallas as pl
from jax.experimental.pallas import tpu as pltpu
from jax.sharding import PartitionSpec as P

MESH = pl.DeviceIdType.MESH
F32 = jnp.float32
BF16 = jnp.bfloat16
FB = 1848
DB = 512
LANES = ((0, 512), (512, 1024), (1024, 1536), (1536, 1848))
N_REMOTE = 112
ORDER = ((1, "y"), (3, "z"), (0, "z"), (2, "y"))
SCALE = 1.0 / 32.0


def nt(a, b):
    return lax.dot_general(a, b, (((1,), (1,)), ((), ())), preferred_element_type=F32)


def nn(a, b):
    return lax.dot_general(a, b, (((1,), (0,)), ((), ())), preferred_element_type=F32)


def tn(a, b):
    return lax.dot_general(a, b, (((0,), (0,)), ((), ())), preferred_element_type=F32)


def kernel(
    tok_in, go_in, gate_in, up_in, wg_in, wu_in, dw_in,
    ot, dwg_out, ou, dwd_out,
    gu, hg, ab, hid, go, tok, gos, dw, dws, wg, wu, part, r1, s1, r2, r3, q1, r4,
    gt, rgx, rgd, sl, rl, og, od, ss, rs, ls,
):
    z = lax.axis_index("gx")
    gy = lax.axis_index("gy")
    gz = lax.axis_index("gz")
    x, l = gy // 2, gy % 2
    h, c = gz // 2, gz % 2
    nc, nh = 1 - c, 1 - h
    other_gy = x * 2 + (1 - l)
    zs = [lax.rem(z + d, 4) for d in range(4)]

    def zdev(d):
        return (zs[d], gy, gz)

    hidev = (z, gy, nh * 2 + c)
    sib = (z, gy, h * 2 + nc)

    def gydev(dx, dl):
        return (z, lax.rem(x + dx, 4) * 2 + lax.rem(l + dl, 2), gz)

    gy_offsets = [(dx, dl) for dx in range(4) for dl in range(2)][1:]

    sent = []

    def remote(src, dst, dev, i):
        return pltpu.make_async_remote_copy(
            src_ref=src, dst_ref=dst, send_sem=ss.at[i], recv_sem=rs.at[i],
            device_id=dev, device_id_type=MESH,
        )

    def send(src, dst, dev):
        copy = remote(src, dst, dev, len(sent))
        copy.start()
        sent.append(copy)
        return copy

    def same(ref, dev):
        return send(ref, ref, dev)

    n_local = [0]

    def local(src, dst):
        copy = pltpu.make_async_copy(src, dst, ls.at[n_local[0]])
        n_local[0] += 1
        copy.start()
        return copy

    l_go = local(go_in, go.at[:, :, gy])
    l_gate = local(gate_in, gu.at[0, c, :, z, h])
    l_up = local(up_in, gu.at[1, c, :, z, h])
    l_dw = local(dw_in, dw)
    l_tok = local(tok_in, tok.at[:, :, gy])
    l_wg = local(wg_in, wg)
    l_wu = local(wu_in, wu)

    peers = [sib, hidev] + [zdev(d) for d in (1, 2, 3)] + [gydev(*o) for o in gy_offsets]
    barrier = pltpu.get_barrier_semaphore()
    for dev in peers:
        pl.semaphore_signal(barrier, inc=1, device_id=dev, device_id_type=MESH)
    pl.semaphore_wait(barrier, len(peers))

    l_go.wait()
    go_lo = same(go.at[:, :, gy], gydev(0, 1))
    go_own = {d: same(go.at[:, :, gy], gydev(d, 0)) for d in (1, 3, 2)}
    l_dw.wait()
    c_dws = send(dw, dws, sib)
    l_gate.wait()
    l_up.wait()
    go_other, gu1_z, gu0_hi, gu1_hi = {}, [], [], []

    def grad_out_2():
        go_lo.wait_recv()
        go_other.update({d: same(go.at[:, :, other_gy], gydev(d, 0)) for d in (1, 3, 2)})

    def gate_up_z():
        gu1_z.extend([same(gu.at[:, c, 1, z, h], zdev(d)) for d in (1, 3)])

    def gate_up_y0():
        gu0_hi.append(same(gu.at[:, c, 0, z, h], hidev))

    def gate_up_y1():
        gu1_hi.append(same(gu.at[:, c, 1, z, h], hidev))

    xts = {d: lax.rem(x + (4 - d), 4) for d in range(4)}
    kind = dict(ORDER)
    slot = {d: [e for e, t in ORDER if t == kind[d]].index(d) for d in kind}
    zk, zh = [v // 2 for v in zs], [v % 2 for v in zs]
    mine = pl.ds(pl.multiple_of(h * 16, 16), 16)
    theirs = pl.ds(pl.multiple_of(nh * 16, 16), 16)
    one, two, spread_one, spread_two, to_sib, gt_copies, gt_last = {}, {}, {}, {}, {}, [], []

    def product(d):
        xt = xts[d]
        pair = pl.ds(xt * 2, 2)
        if d:
            go_own[d].wait_recv()
            go_other[d].wait_recv()
        gos_d = send(go.at[nc, :, pair], gos.at[:, pair], sib)
        gos_d.wait_recv()
        own = go[c, :, pair].reshape(128, DB)
        other = gos[:, pair].reshape(128, DB)
        for a, b in LANES:
            p = nt(own, dw[a:b, :]) + nt(other, dws[a:b, :])
            part[xt, :, :, :, a:b] = p.astype(BF16).reshape(2, 2, 32, b - a)
        if kind[d] == "z":
            one[d] = [send(part.at[xt, zk[e], zh[e]], r1.at[slot[d], e - 1], zdev(e)) for e in (1, 3, 2)]
        else:
            one[d] = [send(part.at[xt, :, :, theirs], r3.at[slot[d]], hidev)]

    def middle(d):
        xt, i = xts[d], slot[d]
        for copy in one[d]:
            copy.wait_recv()
        if kind[d] == "z":
            for a, b in LANES:
                total = part[xt, zk[0], zh[0], :, a:b].astype(F32)
                for e in range(3):
                    total = total + r1[i, e, :, a:b].astype(F32)
                s1[i, :, a:b] = total.astype(BF16)
            two[d] = [send(s1.at[i, theirs], r2.at[i], hidev)]
        else:
            for a, b in LANES:
                total = part[xt, :, :, mine, a:b].astype(F32) + r3[i, :, :, :, a:b].astype(F32)
                q1[i, :, :, :, a:b] = total.astype(BF16)
            two[d] = [send(q1.at[i, zk[e], zh[e]], r4.at[i, e - 1], zdev(e)) for e in (1, 3, 2)]

    def own_sum(d):
        xt, i = xts[d], slot[d]
        for copy in two[d]:
            copy.wait_recv()
        for a, b in LANES:
            if kind[d] == "z":
                total = s1[i, mine, a:b].astype(F32) + r2[i, :, a:b].astype(F32)
            else:
                total = q1[i, zk[0], zh[0], :, a:b].astype(F32)
                for e in range(3):
                    total = total + r4[i, e, :, a:b].astype(F32)
            hg[c, zk[0], xt, zh[0], mine, a:b] = total.astype(BF16)
        block = hg.at[c, zk[0], xt, zh[0], mine]
        if kind[d] == "z":
            spread_one[d] = [same(block, hidev)]
        else:
            spread_one[d] = [same(block, zdev(e)) for e in (1, 2, 3)]
            spread_two[d] = [same(block, hidev)]

    def spread(d):
        xt = xts[d]
        if kind[d] == "z":
            spread_one[d][0].wait_recv()
            pair = hg.at[c, zk[0], xt, zh[0]]
            spread_two[d] = [same(pair, zdev(e)) for e in (1, 2, 3)]
            to_sib[d] = [same(pair, sib)]
        else:
            for e in (1, 2, 3):
                spread_one[d][e - 1].wait_recv()
                spread_two[d].append(same(hg.at[c, zk[4 - e], xt, zh[4 - e], mine], hidev))
            to_sib[d] = [same(hg.at[c, :, xt, :, mine], sib)]

    def last_spread(d):
        xt = xts[d]
        if kind[d] == "z":
            for e in (1, 2, 3):
                spread_two[d][e - 1].wait_recv()
                to_sib[d].append(same(hg.at[c, zk[4 - e], xt, zh[4 - e]], sib))
        else:
            for copy in spread_two[d]:
                copy.wait_recv()
            to_sib[d].append(same(hg.at[c, :, xt, :, theirs], sib))

    def input_grad(d):
        xt = xts[d]
        for copy in to_sib[d]:
            copy.wait_recv()

        def block(i, carry):
            cc, k, hh = i // 4, (i // 2) % 2, i % 2
            for a, b in LANES:
                grad = hg[cc, k, xt, hh, :, a:b]
                ab[0, cc, k, xt, hh, :, a:b] = ab[0, cc, k, xt, hh, :, a:b] * grad
                ab[1, cc, k, xt, hh, :, a:b] = ab[1, cc, k, xt, hh, :, a:b] * grad
            return carry

        lax.fori_loop(0, 8, block, 0)
        term = nn(ab[0, :, :, xt].reshape(256, FB), wg[...])
        term = term + nn(ab[1, :, :, xt].reshape(256, FB), wu[...])
        term = term.astype(BF16).reshape(2, 2, 2, 32, DB)
        for hh in range(2):
            gt[xt, hh] = term[:, :, hh]
        if d == ORDER[-1][0]:
            gt_last.append(send(gt.at[xt, l], rgd.at[0], (z, xt * 2 + l, gz)))
            gt_last.append(send(gt.at[xt, 1 - l], rgd.at[1], (z, xt * 2 + 1 - l, gz)))
        elif d:
            gt_copies.append(send(gt.at[xt], rgx.at[len(gt_copies)], (z, xt * 2 + l, gz)))

    def pointwise(cc, k, part_of):
        def block(i, carry):
            zz, hh = i // 2, i % 2
            for a, b in LANES:
                gate = gu[0, cc, k, zz, hh, :, a:b].astype(F32)
                up = gu[1, cc, k, zz, hh, :, a:b].astype(F32)
                s = 0.5 + 0.5 * jnp.tanh(0.5 * gate)
                silu = gate * s
                ab[0, cc, k, zz, hh, :, a:b] = (up * (s * (1.0 + gate - silu))).astype(BF16)
                ab[1, cc, k, zz, hh, :, a:b] = silu.astype(BF16)
                hid[cc, k, zz, hh, :, a:b] = (silu * up).astype(BF16)
            return carry

        lax.fori_loop(4 * part_of, 4 * part_of + 4, block, 0)

    gu1_f, gu0_z, gu0_f, gu_s, tok_lo, tok_x, lo_sum, stores = [], [], [], {}, [], [], [], []

    def gate_up_1():
        gu1_z[0].wait_recv()
        gu1_f.append(same(gu.at[0, c, 1, zs[3], h], zdev(1)))
        gu1_z[1].wait_recv()
        gu1_f.append(same(gu.at[1, c, 1, zs[1], h], zdev(3)))

    def gate_up_2():
        gu0_hi[0].wait_recv()
        gu0_z.extend([same(gu.at[:, c, 0, z], zdev(d)) for d in (1, 3)])

    def gate_up_3():
        gu1_hi.extend([same(gu.at[:, c, 1, zs[d], h], hidev) for d in (1, 3)])

    def gate_up_4():
        for copy in gu1_f:
            copy.wait_recv()
        gu1_hi.append(same(gu.at[:, c, 1, zs[2], h], hidev))
        gu_s[0] = same(gu.at[:, c, 1, :, h], sib)

    def gate_up_5():
        gu0_z[0].wait_recv()
        gu0_f.append(same(gu.at[0, c, 0, zs[3]], zdev(1)))
        gu0_z[1].wait_recv()
        gu0_f.append(same(gu.at[1, c, 0, zs[1]], zdev(3)))

    def gate_up_6():
        for copy in gu1_hi:
            copy.wait_recv()
        gu_s[1] = same(gu.at[:, c, 1, :, nh], sib)

    def gate_up_7():
        for copy in gu0_f:
            copy.wait_recv()
        gu_s[2] = same(gu.at[:, c, 0], sib)

    def tokens_1():
        l_tok.wait()
        tok_lo.append(same(tok.at[:, :, gy], gydev(0, 1)))
        tok_x.extend([same(tok.at[:, :, gy], gydev(d, 0)) for d in (1, 2, 3)])

    def tokens_2():
        tok_lo[0].wait_recv()
        tok_x.extend([same(tok.at[:, :, other_gy], gydev(d, 0)) for d in (1, 2, 3)])

    def sum_lo():
        for copy in gt_copies:
            copy.wait_recv()
        for cc in range(2):
            total = gt[x, 1 - l, cc].astype(F32) + rgx[0, 1 - l, cc].astype(F32) + rgx[1, 1 - l, cc].astype(F32)
            sl[cc] = total.astype(BF16)
        gt_last.append(send(sl, rl, gydev(0, 1)))

    def down_grad():
        for a, b in LANES:
            w = tn(hid[:, :, :, :, :, a:b].reshape(1024, b - a), go[...].reshape(1024, DB))
            od[a:b, :] = (w * SCALE).astype(BF16)
        stores.append(local(od, dwd_out))

    gate_up_z()
    gate_up_y0()
    gate_up_1()
    gate_up_3()
    grad_out_2()
    gate_up_2()
    gate_up_4()
    c_dws.wait_recv()
    product(1)
    product(3)
    gate_up_5()
    gate_up_y1()
    product(2)
    middle(3)
    middle(1)
    product(0)
    own_sum(1)
    gu_s[0].wait_recv()
    gate_up_7()
    own_sum(3)
    gate_up_6()
    tokens_1()
    pointwise(c, 0, 1)
    middle(2)
    middle(0)
    pointwise(c, 1, 0)
    gu_s[2].wait_recv()
    gu_s[1].wait_recv()
    spread(1)
    spread(3)
    pointwise(nc, 0, 1)
    pointwise(c, 1, 1)
    own_sum(0)
    pointwise(nc, 1, 1)
    own_sum(2)
    pointwise(nc, 1, 0)
    pointwise(c, 0, 0)
    tokens_2()
    spread(0)
    last_spread(1)
    pointwise(nc, 0, 0)
    last_spread(3)
    spread(2)
    l_wg.wait()
    l_wu.wait()
    input_grad(1)
    input_grad(3)
    last_spread(0)
    last_spread(2)
    input_grad(2)
    input_grad(0)
    sum_lo()
    down_grad()
    for copy in tok_x:
        copy.wait_recv()

    for which, out in enumerate((og, ou)):
        for a, b in LANES:
            grads = ab[which, :, :, :, :, :, a:b].reshape(1024, b - a)
            w = tn(grads, tok[...].reshape(1024, DB))
            out[a:b, :] = (w * SCALE).astype(BF16)
        if which == 0:
            stores.append(local(og, dwg_out))

    for copy in gt_last:
        copy.wait_recv()
    for cc in range(2):
        total = gt[x, l, cc].astype(F32) + rl[cc].astype(F32)
        for j in range(2):
            total = total + rgx[j, l, cc].astype(F32) + rgd[j, cc].astype(F32)
        ot[cc] = total.astype(BF16)
    for copy in sent:
        copy.wait_send()
    for copy in stores:
        copy.wait()
    assert len(sent) <= N_REMOTE


def copy_kernel(gt_in, dwg_in, dwu_in, dwd_in, gt_out, dwg_out, dwu_out, dwd_out, held_g, held_d, sems):
    reads = [
        pltpu.make_async_copy(dwg_in, held_g, sems.at[0]),
        pltpu.make_async_copy(dwd_in, held_d, sems.at[1]),
    ]
    writes = [
        pltpu.make_async_copy(held_g, dwg_out, sems.at[2]),
        pltpu.make_async_copy(held_d, dwd_out, sems.at[3]),
        pltpu.make_async_copy(gt_in, gt_out, sems.at[4]),
        pltpu.make_async_copy(dwu_in, dwu_out, sems.at[5]),
    ]
    for copy in reads + writes[2:]:
        copy.start()
    for read, write in zip(reads, writes):
        read.wait()
        write.start()
    for copy in writes:
        copy.wait()


def local_step(tokens, grad_out, gate_pre, up_pre, gate_weight, up_weight, down_weight):
    any_spec = pl.BlockSpec(memory_space=pl.ANY)
    vm = pltpu.VMEM
    vm_spec = pl.BlockSpec(memory_space=vm)
    outs = pl.pallas_call(
        kernel,
        out_shape=(
            vm((2, 2, 32, DB), BF16),
            jax.ShapeDtypeStruct((FB, DB), BF16),
            vm((FB, DB), BF16),
            jax.ShapeDtypeStruct((FB, DB), BF16),
        ),
        in_specs=[any_spec] * 7,
        out_specs=(vm_spec, any_spec, vm_spec, any_spec),
        scratch_shapes=[
            vm((2, 2, 2, 4, 2, 32, FB), BF16),
            vm((2, 2, 4, 2, 32, FB), BF16),
            vm((2, 2, 2, 4, 2, 32, FB), BF16),
            vm((2, 2, 4, 2, 32, FB), BF16),
            vm((2, 2, 8, 32, DB), BF16),
            vm((2, 2, 8, 32, DB), BF16),
            vm((2, 8, 32, DB), BF16),
            vm((FB, DB), BF16),
            vm((FB, DB), BF16),
            vm((FB, DB), BF16),
            vm((FB, DB), BF16),
            vm((4, 2, 2, 32, FB), BF16),
            vm((4, 3, 32, FB), BF16),
            vm((4, 32, FB), BF16),
            vm((4, 16, FB), BF16),
            vm((4, 2, 2, 16, FB), BF16),
            vm((4, 2, 2, 16, FB), BF16),
            vm((4, 3, 16, FB), BF16),
            vm((4, 2, 2, 2, 32, DB), BF16),
            vm((2, 2, 2, 2, 32, DB), BF16),
            vm((2, 2, 2, 32, DB), BF16),
            vm((2, 2, 32, DB), BF16),
            vm((2, 2, 32, DB), BF16),
            vm((FB, DB), BF16),
            vm((FB, DB), BF16),
            pltpu.SemaphoreType.DMA((N_REMOTE,)),
            pltpu.SemaphoreType.DMA((N_REMOTE,)),
            pltpu.SemaphoreType.DMA((16,)),
        ],
        compiler_params=pltpu.CompilerParams(
            collective_id=0, has_side_effects=True, vmem_limit_bytes=60 * 1024 * 1024
        ),
        name="swiglu_backward",
    )(
        tokens.reshape(2, 2, 32, DB),
        grad_out.reshape(2, 2, 32, DB),
        gate_pre.reshape(2, 32, FB),
        up_pre.reshape(2, 32, FB),
        gate_weight.T,
        up_weight.T,
        down_weight,
    )
    outs = pl.pallas_call(
        copy_kernel,
        out_shape=tuple(jax.ShapeDtypeStruct(o.shape, o.dtype) for o in outs),
        in_specs=[vm_spec, any_spec, vm_spec, any_spec],
        out_specs=(any_spec,) * 4,
        scratch_shapes=[vm((FB, DB), BF16)] * 2 + [pltpu.SemaphoreType.DMA((6,))],
        name="hand_out",
    )(
        pltpu.with_memory_space_constraint(outs[0], vm),
        outs[1],
        pltpu.with_memory_space_constraint(outs[2], vm),
        outs[3],
    )
    return (outs[0].reshape(128, DB), outs[1].T, outs[2].T, outs[3])


def solution(mesh):
    return jax.shard_map(
        local_step,
        mesh=mesh,
        in_specs=(
            P("gy", ("gx", "gz")),
            P("gy", ("gx", "gz")),
            P(("gx", "gz"), "gy"),
            P(("gx", "gz"), "gy"),
            P(("gx", "gz"), "gy"),
            P(("gx", "gz"), "gy"),
            P("gy", ("gx", "gz")),
        ),
        out_specs=(
            P("gy", ("gx", "gz")),
            P(("gx", "gz"), "gy"),
            P(("gx", "gz"), "gy"),
            P("gy", ("gx", "gz")),
        ),
        check_vma=False,
    )
```
